256 devices in a mesh: forest: 8 (over x, core), tile: 32 (over z, y).
Axes of the slice: x: 4, y: 4, z: 8, core: 2. Of those that a mesh axis runs over, the one named last changes fastest.
Arguments:
- left_panels: bfloat16 [8, 256, 2, 256, 256], P('forest', 'tile'), may hold values from -4 to 4
- right_panels: bfloat16 [8, 256, 1, 256, 256], P('forest', 'tile'), may hold values from -0.375 to 0.375
- dest_owner: int32 [8, 256, 1], P('forest', 'tile'), may hold values from 0 to 31; in each aligned block of 8 rows (0 to 7, 8 to 15, ..., all dimensions but the last counted through in order) at most 2 rows name the same one
- tile_slot: int32 [8, 256], P('forest', 'tile'), may hold values from 0 to 1
- frontal_tiles: float32 [64, 2, 256, 256], P('tile', None, 'forest'), may hold values from -6 to 6
- diag_inverse: float32 [256, 256], replicated, as said below
- reader_tile: int32 [128], replicated, may hold values from 0 to 63
Outputs:
- ancestor: float32 [64, 2, 256, 256], P('tile', None, 'forest')
- panel_read: float32 [128, 2, 256, 256], P('tile', None, 'forest')
The draws below stay inside these ranges and needn't reach their ends.
Inputs may be any that keep to these rules, and one draw needn't show every extreme that they name: `dest_owner`: among the pairs of one device at most 2 name the same owner, and some device has exactly 2 for one owner. `diag_inverse`: an upper triangular matrix with a positive diagonal.
All inputs are finite; a program needn't handle non-finite values.
Results may differ from the reference program's by a relative error of at most 0.0003.
Values may be sent and summed in bfloat16 or wider, within the bound.
A program may use at most 192 MiB of HBM per device.

```python
import math
import jax
import jax.numpy as jnp
import numpy as np
from jax import lax

B = 256
R = 2
C = 1
PAIRS = 8
TILES_DEV = 2
READS = 4
CAP = 2
TILES = 64
N_FOREST = 8
N_TILE = 32


def draw_diag_inverse(key, part):
    key_off = jax.random.fold_in(key, 11)
    key_diag = jax.random.fold_in(key, 12)
    off_diagonal = jax.random.normal(key_off, (B, B), jnp.float32) * (0.5 / math.sqrt(B))
    diagonal = jax.random.uniform(key_diag, (B,), jnp.float32, 0.7, 1.4)
    return jnp.triu(off_diagonal, 1) + jnp.diag(diagonal)


def set_ends(result, rng, least, largest):
    spot = [jax.random.randint(jax.random.fold_in(rng, axis), (), 0, length) for axis, length in enumerate(result.shape)]
    main_axis = result.shape.index(max(result.shape))
    neighbour = spot[:main_axis] + [(spot[main_axis] + 1) % result.shape[main_axis]] + spot[main_axis + 1:]
    return result.at[tuple(spot)].set(least).at[tuple(neighbour)].set(largest)


def shard_levels(rng, shape, shards, least, largest):
    def one(axis_at, blocks):
        draws = jax.random.uniform(jax.random.fold_in(jax.random.fold_in(rng, 6), axis_at), (blocks,), jnp.float32, least / len(shards), largest / len(shards))
        return jnp.repeat(jnp.exp(draws), shape[axis_at] // blocks).reshape((-1,) + (1,) * (len(shape) - axis_at - 1))

    gain = one(*shards[0])
    for cut in shards[1:]:
        gain = gain * one(*cut)
    return gain


def assign_block(rng, own, number, rows, count, top, reach, skew):
    sequence = jax.random.permutation(rng, count)
    packed, ordinary = shares(count, rows * top, reach, skew, True), shares(count, rows * top, reach, skew, False)
    places = jnp.arange(count)

    def named(tallies, offset_by):
        used = int((tallies > 0).sum())
        fixed = max(1, used // 4)
        moved = fixed + (places - fixed + offset_by * (used - fixed)) % max(1, count - fixed)
        return jnp.zeros((count,), jnp.int32).at[sequence[jnp.where(places < fixed, places, moved)]].set(jnp.asarray(tallies, jnp.int32))

    tallies = jnp.where(number % 4 == 0, named(packed, number // 4), named(ordinary, number - number // 4 - 1))
    mixed = jax.random.permutation(jax.random.fold_in(own, 3), count)
    source_of, receiver = mixed[0:count // 2 * 2:2], mixed[1:count // 2 * 2:2]
    slack = jnp.minimum(tallies[source_of] - 1, reach - tallies[receiver]) // 2
    slack = jnp.where((source_of == sequence[0]) | (receiver == sequence[0]) | (tallies[receiver] == 0), 0, jnp.maximum(slack, 0))
    moved = jax.random.randint(jax.random.fold_in(own, 4), (count // 2,), 0, 1 << 20) % (slack + 1)
    tallies = tallies.at[source_of].add(-moved).at[receiver].add(moved)
    items = jnp.searchsorted(jnp.cumsum(tallies), jnp.arange(rows * top), side="right").astype(jnp.int32)
    grid = items.reshape(top, rows).T
    grid = grid[jax.random.permutation(jax.random.fold_in(own, 1), rows)]
    offset_by = jax.random.randint(jax.random.fold_in(own, 2), (rows, 1), 0, top)
    return jnp.take_along_axis(grid, (jnp.arange(top)[None, :] + offset_by) % top, axis=1)


def shares(number_of, total, reach, slope, full):
    weights = [(1 << 20) // math.isqrt(standing ** slope) + 1 for standing in range(1, number_of + 1)]
    largest = reach if full else min(reach, max(-(-total // number_of), total * weights[0] // sum(weights)))
    least = 1 if total - largest >= number_of - 1 else 0
    counts, spare = [largest] + [least] * (number_of - 1), total - largest - least * (number_of - 1)
    while spare > 0:
        free = [i for i in range(1, number_of) if counts[i] < largest] or [i for i in range(1, number_of) if counts[i] < reach]
        mass, budget = sum([weights[i] for i in free]), spare
        for i in free:
            extra = min(reach - counts[i], max(1, budget * weights[i] // mass), spare)
            counts[i] = counts[i] + extra
            spare = spare - extra
    return np.array(counts)


def normal_values(key, shape, deviation, reach, cuts=(), held_as=jnp.bfloat16):
    result = deviation * jax.random.normal(key, shape, jnp.float32)
    if cuts:
        result = result * shard_levels(key, shape, cuts, -0.22, 0.18)
    return jnp.clip(result, -reach, reach).astype(held_as)


def setup_inputs(seed: int = 0) -> dict:
    arg_keys = jax.random.split(jax.random.key(seed), 8)
    left_panels = normal_values(arg_keys[0], (N_FOREST, N_TILE * PAIRS, R, B, B), 0.25, 4.0, ((0, 8), (1, 32)))
    right_panels = normal_values(arg_keys[1], (N_FOREST, N_TILE * PAIRS, C, B, B), B ** -0.5, 0.375, ((0, 8), (1, 32)))
    dest_owner_keys = jax.random.split(jax.random.fold_in(arg_keys[2], 1), N_FOREST * (N_TILE * PAIRS) // PAIRS)
    dest_owner_turns = jax.random.permutation(jax.random.fold_in(arg_keys[2], 3), N_FOREST * (N_TILE * PAIRS) // PAIRS)
    dest_owner = jax.vmap(lambda own, number: assign_block(jax.random.fold_in(arg_keys[2], 2), own, number, PAIRS, N_TILE, 1, CAP, 2))(dest_owner_keys, dest_owner_turns).reshape((N_FOREST, N_TILE * PAIRS, 1))
    tile_slot = set_ends(jax.random.randint(arg_keys[3], (N_FOREST, N_TILE * PAIRS), 0, TILES_DEV), jax.random.fold_in(arg_keys[3], 1), 0, TILES_DEV - 1).astype(jnp.int32)
    frontal_tiles = normal_values(arg_keys[4], (TILES, R * C, B, B), 1.0, 6.0, ((0, 32), (2, 8)), jnp.float32)
    diag_inverse = draw_diag_inverse(jax.random.fold_in(arg_keys[7], 71), 0)
    reader_tile = set_ends(jax.random.randint(arg_keys[6], (N_TILE * READS,), 0, TILES), jax.random.fold_in(arg_keys[6], 1), 0, TILES - 1).astype(jnp.int32)
    return dict(left_panels=left_panels, right_panels=right_panels, dest_owner=dest_owner, tile_slot=tile_slot, frontal_tiles=frontal_tiles, diag_inverse=diag_inverse, reader_tile=reader_tile)


def reference(left_panels, right_panels, dest_owner, tile_slot, frontal_tiles, diag_inverse, reader_tile):
    tile_total = N_TILE * TILES_DEV

    def one_grid(running, grid_data):
        left_block, right_block, owners, slot_index = grid_data
        products = jnp.einsum("kaij,kcjl->kacil", left_block.astype(jnp.float32), right_block.astype(jnp.float32), precision=lax.Precision.HIGHEST)
        products = products.reshape(products.shape[0], R * C, B, B) / R
        target_tile = (owners[:, 0] * TILES_DEV + slot_index).astype(jnp.int32)
        return running.at[target_tile].add(products), None

    updates, _ = lax.scan(one_grid, jnp.zeros((tile_total, R * C, B, B), jnp.float32), (left_panels, right_panels, dest_owner, tile_slot))
    schur_tile = frontal_tiles - updates
    panel_tile = jnp.einsum("qtrj,jk->qtrk", schur_tile, diag_inverse, precision=lax.Precision.HIGHEST)
    return schur_tile, jnp.take(panel_tile, reader_tile.astype(jnp.int32), axis=0)
```

```python
import jax
import jax.numpy as jnp
from jax import lax
from jax.sharding import PartitionSpec as P


def per_device(
    left_panels, right_panels, dest_owner, tile_slot, frontal_tiles, diag_inverse, reader_tile
):
    forest_count = lax.axis_size("forest")
    tile_count = lax.axis_size("tile")
    per_dev = frontal_tiles.shape[0]
    group_count = tile_count * per_dev
    left_block = left_panels[0]
    right_block = right_panels[0, :, 0]
    pairs, depth, width = left_block.shape[:3]
    rows = width // forest_count
    group = dest_owner[0, :, 0] * per_dev + tile_slot[0]

    with jax.named_scope("products"):
        products = jnp.einsum(
            "kaij,kjl->kail", left_block, right_block, preferred_element_type=jnp.float32
        )
        products = products.reshape(pairs, depth, forest_count, rows, width)
        products = products.transpose(2, 0, 1, 3, 4)
    with jax.named_scope("to_row_owners"):
        groups = lax.all_gather(group, "forest", axis=0, tiled=True)
        pieces = lax.all_to_all(products, "forest", split_axis=0, concat_axis=0, tiled=True)
    with jax.named_scope("sum_by_group"):
        pieces = pieces.reshape(forest_count * pairs, depth * rows * width)
        hot = jnp.where(
            groups[None, :] == jnp.arange(group_count, dtype=jnp.int32)[:, None], 1.0 / depth, 0.0
        ).astype(jnp.float32)
        updates = jnp.dot(hot, pieces, precision=lax.Precision.HIGHEST)
        updates = updates.reshape(group_count, depth, rows, width)
        reduced = lax.psum_scatter(updates, "tile", scatter_dimension=0, tiled=True)
    with jax.named_scope("solve"):
        ancestor = frontal_tiles - reduced
        panel = jnp.einsum(
            "qtrj,jk->qtrk", ancestor, diag_inverse, precision=lax.Precision.HIGHEST
        )
    with jax.named_scope("reads"):
        gathered = lax.all_gather(panel, "tile", axis=0, tiled=True)
        reads = reader_tile.shape[0] // tile_count
        first = lax.axis_index("tile") * reads
        picked = []
        for i in range(reads):
            at = lax.dynamic_index_in_dim(reader_tile, first + i, 0, keepdims=False)
            picked.append(lax.dynamic_slice_in_dim(gathered, at, 1, 0))
        picked = jnp.concatenate(picked, axis=0)
    return ancestor, picked


def solution(mesh):
    placed = (
        P("forest", "tile", None, None, None),
        P("forest", "tile", None, None, None),
        P("forest", "tile", None),
        P("forest", "tile"),
        P("tile", None, "forest", None),
        P(),
        P(),
    )
    return jax.shard_map(
        per_device,
        mesh=mesh,
        in_specs=placed,
        out_specs=(P("tile", None, "forest", None), P("tile", None, "forest", None)),
        check_vma=False,
    )
```

```python
import functools

import jax
import jax.numpy as jnp
from jax import lax
from jax.experimental import pallas as pl
from jax.experimental.pallas import tpu as pltpu
from jax.sharding import PartitionSpec as P

MESH = pl.DeviceIdType.MESH
Y = 4
Z = 8
F = 8
CHUNKS = 2
TOP = 32767.0


def encode(v):
    most = jnp.maximum(jnp.max(jnp.abs(v), axis=0, keepdims=True), 1e-30)
    q = jnp.round(v * (TOP / most)).astype(jnp.int32).astype(jnp.int16)
    return q, most * (1.0 / TOP)


def decode(q, scale):
    return q.astype(jnp.int32).astype(jnp.float32) * scale


def kernel(owner, slot, reads, left, right, frontal, inverse, ancestor, picked, *scratch):
    (ids, meta_v, meta, x_out, xs_out, x_in, xs_in, y_out, ys_out, y_in, ys_in,
     z_out, zs_out, z_in, zs_in, total, r_out, rs_out, *rest) = scratch
    sums, rest = rest[:CHUNKS], rest[CHUNKS:]
    g_all, rest = rest[:CHUNKS], rest[CHUNKS:]
    gs_all, rest = rest[:CHUNKS], rest[CHUNKS:]
    r_all, rest = rest[:CHUNKS], rest[CHUNKS:]
    rs_all, rest = rest[:CHUNKS], rest[CHUNKS:]
    id_sem, x_sem, y_sem, z_sem, g_sem, r_sem, own_sem, meta_sem = rest

    pairs, depth, width = left.shape[:3]
    rows = width // F
    part = depth * rows // CHUNKS
    cuts = rows // part
    per_dev = frontal.shape[0]
    listed = picked.shape[0]
    f = lax.axis_index("forest")
    t = lax.axis_index("tile")
    z, y = t // Y, t % Y

    forest_peers = [((f + i) % F, t) for i in range(1, F)]
    y_peers = [(f, z * Y + (y + i) % Y) for i in range(1, Y)]
    z_peers = [(f, (z + i) % Z * Y + y) for i in range(1, Z)]
    barrier = pltpu.get_barrier_semaphore()
    for peer in forest_peers + y_peers + z_peers:
        pl.semaphore_signal(barrier, inc=1, device_id=peer, device_id_type=MESH)

    def send(src, dst, sems, at, peer):
        copy = pltpu.make_async_remote_copy(
            src_ref=src, dst_ref=dst, send_sem=sems.at[(0,) + at], recv_sem=sems.at[(1,) + at],
            device_id=peer, device_id_type=MESH,
        )
        copy.start()
        return copy

    lane = lax.broadcasted_iota(jnp.int32, (8, 128), 1)
    sub = lax.broadcasted_iota(jnp.int32, (8, 128), 0)
    down = jnp.zeros((8, 128), jnp.int32)
    along = jnp.zeros((8, 128), jnp.int32)
    for k in range(pairs):
        group = owner[k] * per_dev + slot[k]
        down = jnp.where(sub == k, group, down)
        along = jnp.where(lane == f * pairs + k, group, along)
    ids[f, 0:8, :] = down
    ids[f, 8:16, :] = along

    def products(c):
        tile, cut = c // cuts, c % cuts

        def body(k, carry):
            a = left[k, tile].reshape(F, rows, width)[:, cut * part:(cut + 1) * part]
            out = jnp.dot(
                a.reshape(F * part, width), right[k, 0], preferred_element_type=jnp.float32
            )
            for d in range(F):
                q, s = encode(out[d * part:(d + 1) * part])
                x_out[d, c, k] = q
                xs_out[d, c, k] = s
            return carry

        lax.fori_loop(0, pairs, body, 0)

    sent = []
    x_copies = {}
    for c in range(CHUNKS):
        products(c)
        if c == 0:
            pl.semaphore_wait(barrier, len(forest_peers + y_peers + z_peers))
            id_copies = [
                send(ids.at[f], ids.at[f], id_sem, (i,), peer)
                for i, peer in enumerate(forest_peers)
            ]
            sent += id_copies
        x_copies[c] = []
        for i, peer in enumerate(forest_peers):
            d = peer[0]
            x_copies[c].append(send(x_out.at[d, c], x_in.at[f, c], x_sem, (0, c, i), peer))
            x_copies[c].append(send(xs_out.at[d, c], xs_in.at[f, c], x_sem, (1, c, i), peer))
        sent += x_copies[c]
        own = [
            pltpu.make_async_copy(x_out.at[f, c], x_in.at[f, c], own_sem.at[0]),
            pltpu.make_async_copy(xs_out.at[f, c], xs_in.at[f, c], own_sem.at[1]),
        ]
        for copy in own:
            copy.start()
        for copy in own:
            copy.wait()

    for copy in id_copies:
        copy.wait_recv()
    count = F * pairs
    cols = ids[:, 0:8, :].reshape(count, 128)
    line = jnp.sum(ids[:, 8:16, :], axis=0)
    line = jnp.broadcast_to(line[None], (F, 8, 128)).reshape(count, 128)
    number = lax.broadcasted_iota(jnp.int32, (count, 128), 0)
    place = lax.broadcasted_iota(jnp.int32, (count, 128), 1)

    def latest(mask):
        at = jnp.max(jnp.where(mask, number, -1), axis=0, keepdims=True)
        return jnp.broadcast_to(jnp.where(at < 0, count, at), (8, 128))

    meta_v[0:8, :] = latest((cols == line) & (number < place))
    meta_v[8:16, :] = latest(cols == place)
    copy = pltpu.make_async_copy(meta_v, meta, meta_sem)
    copy.start()
    copy.wait()

    y_copies = {}
    for c in range(CHUNKS):
        for copy in x_copies[c]:
            copy.wait_recv()
        held = sums[c]
        held[count] = jnp.zeros((part, width), jnp.float32)

        def chain(j, carry, c=c, held=held):
            v = decode(x_in[j // pairs, c, j % pairs], xs_in[j // pairs, c, j % pairs])
            held[j] = v + held[meta[0, j]]
            return carry

        lax.fori_loop(0, count, chain, 0)
        y_copies[c] = []
        for i, peer in enumerate(y_peers):
            to = (y + i + 1) % Y

            def pack(m, carry, c=c, held=held, i=i, to=to):
                g = (m // per_dev * Y + to) * per_dev + m % per_dev
                q, s = encode(held[meta[8, g]])
                y_out[i, c, m] = q
                ys_out[i, c, m] = s
                return carry

            lax.fori_loop(0, Z * per_dev, pack, 0)
            y_copies[c].append(send(y_out.at[i, c], y_in.at[i, c], y_sem, (0, c, i), peer))
            y_copies[c].append(send(ys_out.at[i, c], ys_in.at[i, c], y_sem, (1, c, i), peer))
        sent += y_copies[c]

    z_copies = {}
    for c in range(CHUNKS):
        for copy in y_copies[c]:
            copy.wait_recv()
        held = sums[c]

        def merge(m, carry, c=c, held=held):
            g = (m // per_dev * Y + y) * per_dev + m % per_dev
            v = held[meta[8, g]]
            for i in range(Y - 1):
                v = v + decode(y_in[i, c, m], ys_in[i, c, m])
            total[c, m] = v
            q, s = encode(v)
            z_out[m // per_dev, c, m % per_dev] = q
            zs_out[m // per_dev, c, m % per_dev] = s
            return carry

        lax.fori_loop(0, Z * per_dev, merge, 0)
        z_copies[c] = []
        for i, peer in enumerate(z_peers):
            to = (z + i + 1) % Z
            z_copies[c].append(send(z_out.at[to, c], z_in.at[i, c], z_sem, (0, c, i), peer))
            z_copies[c].append(send(zs_out.at[to, c], zs_in.at[i, c], z_sem, (1, c, i), peer))
        sent += z_copies[c]

    g_copies = {}
    for c in range(CHUNKS):
        tile, cut = c // cuts, c % cuts
        for copy in z_copies[c]:
            copy.wait_recv()
        for s in range(per_dev):
            v = total[c, z * per_dev + s]
            for i in range(Z - 1):
                v = v + decode(z_in[i, c, s], zs_in[i, c, s])
            v = frontal[s, tile, cut * part:(cut + 1) * part] - v * (1.0 / depth)
            ancestor[s, tile, cut * part:(cut + 1) * part] = v
            solved = jnp.dot(
                v, inverse[...], precision=lax.Precision.HIGHEST,
                preferred_element_type=jnp.float32,
            )
            q, scale = encode(solved)
            g_all[c][z, s] = q
            gs_all[c][z, s] = scale
        g_copies[c] = []
        for i, peer in enumerate(z_peers):
            g_copies[c].append(send(g_all[c].at[z], g_all[c].at[z], g_sem, (0, c, i), peer))
            g_copies[c].append(send(gs_all[c].at[z], gs_all[c].at[z], g_sem, (1, c, i), peer))
        sent += g_copies[c]

    r_copies = {}
    for c in range(CHUNKS):
        for copy in g_copies[c]:
            copy.wait_recv()
        r_copies[c] = []
        for i in range(Y):
            to = (y + i) % Y
            for r in range(listed):
                g = reads[(z * Y + to) * listed + r]
                q = g_all[c][g // (Y * per_dev), g % per_dev]
                scale = gs_all[c][g // (Y * per_dev), g % per_dev]
                if i == 0:
                    r_all[c][y, r] = q
                    rs_all[c][y, r] = scale
                else:
                    r_out[i - 1, c, r] = q
                    rs_out[i - 1, c, r] = scale
            if i:
                peer = y_peers[i - 1]
                r_copies[c].append(
                    send(r_out.at[i - 1, c], r_all[c].at[y], r_sem, (0, c, i - 1), peer)
                )
                r_copies[c].append(
                    send(rs_out.at[i - 1, c], rs_all[c].at[y], r_sem, (1, c, i - 1), peer)
                )
        sent += r_copies[c]

    for c in range(CHUNKS):
        tile, cut = c // cuts, c % cuts
        for copy in r_copies[c]:
            copy.wait_recv()
        for r in range(listed):
            at = reads[t * listed + r] // per_dev % Y
            picked[r, tile, cut * part:(cut + 1) * part] = decode(r_all[c][at, r], rs_all[c][at, r])

    for copy in sent:
        copy.wait_send()


def per_device(
    left_panels, right_panels, dest_owner, tile_slot, frontal_tiles, diag_inverse, reader_tile
):
    left = left_panels[0]
    right = right_panels[0]
    pairs, depth, width = left.shape[:3]
    per_dev = frontal_tiles.shape[0]
    tiles = lax.axis_size("tile")
    listed = reader_tile.shape[0] // tiles
    part = depth * (width // F) // CHUNKS
    count = F * pairs
    mine = Z * per_dev

    def block(*lead):
        return [
            pltpu.VMEM(lead + (part, width), jnp.int16),
            pltpu.VMEM(lead + (1, width), jnp.float32),
        ]

    n = CHUNKS
    scratch = [
        pltpu.VMEM((F, 16, 128), jnp.int32),
        pltpu.VMEM((16, 128), jnp.int32),
        pltpu.SMEM((16, 128), jnp.int32),
        *block(F, n, pairs),
        *block(F, n, pairs),
        *block(Y - 1, n, mine),
        *block(Y - 1, n, mine),
        *block(Z, n, per_dev),
        *block(Z - 1, n, per_dev),
        pltpu.VMEM((n, mine, part, width), jnp.float32),
        *block(Y - 1, n, listed),
        *[pltpu.VMEM((count + 1, part, width), jnp.float32)] * n,
        *[block(Z, per_dev)[0]] * n,
        *[block(Z, per_dev)[1]] * n,
        *[block(Y, listed)[0]] * n,
        *[block(Y, listed)[1]] * n,
        pltpu.SemaphoreType.DMA((2, F - 1)),
        pltpu.SemaphoreType.DMA((2, 2, n, F - 1)),
        pltpu.SemaphoreType.DMA((2, 2, n, Y - 1)),
        pltpu.SemaphoreType.DMA((2, 2, n, Z - 1)),
        pltpu.SemaphoreType.DMA((2, 2, n, Z - 1)),
        pltpu.SemaphoreType.DMA((2, 2, n, Y - 1)),
        pltpu.SemaphoreType.DMA((2,)),
        pltpu.SemaphoreType.DMA,
    ]
    smem = pl.BlockSpec(memory_space=pltpu.SMEM)
    vmem = pl.BlockSpec(memory_space=pltpu.VMEM)
    return pl.pallas_call(
        kernel,
        out_shape=(
            jax.ShapeDtypeStruct(frontal_tiles.shape, jnp.float32),
            jax.ShapeDtypeStruct((listed,) + frontal_tiles.shape[1:], jnp.float32),
        ),
        in_specs=[smem, smem, smem, vmem, vmem, vmem, vmem],
        out_specs=(vmem, vmem),
        scratch_shapes=scratch,
        compiler_params=pltpu.CompilerParams(
            collective_id=0, has_side_effects=True, vmem_limit_bytes=48 << 20
        ),
        cost_estimate=pl.CostEstimate(
            flops=2 * pairs * depth * width**3, bytes_accessed=4 << 20, transcendentals=0
        ),
        name="schur_update",
    )(dest_owner[0, :, 0], tile_slot[0], reader_tile, left, right, frontal_tiles, diag_inverse)


def solution(mesh):
    placed = (
        P("forest", "tile", None, None, None),
        P("forest", "tile", None, None, None),
        P("forest", "tile", None),
        P("forest", "tile"),
        P("tile", None, "forest", None),
        P(),
        P(),
    )
    return jax.shard_map(
        per_device,
        mesh=mesh,
        in_specs=placed,
        out_specs=(P("tile", None, "forest", None), P("tile", None, "forest", None)),
        check_vma=False,
    )
```

```python
import functools

import jax
import jax.numpy as jnp
from jax import lax
from jax.experimental import pallas as pl
from jax.experimental.pallas import tpu as pltpu
from jax.sharding import PartitionSpec as P

MESH = pl.DeviceIdType.MESH
Y = 4
Z = 8
F = 8
HALF = 128
CUTS = 1
CHUNKS = 2 * CUTS
TOP = 32767.0


def scale_of(v):
    v = jnp.abs(v)
    most = functools.reduce(jnp.maximum, [v[i:i + 8] for i in range(0, v.shape[0], 8)])
    most = jnp.maximum(jnp.max(most, axis=0, keepdims=True), 1e-30)
    return most * (1.0 / TOP), TOP / most


def encode(v):
    step, back = scale_of(v)
    return jnp.round(v * back).astype(jnp.int32).astype(jnp.int16), step


def decode(q, step):
    return q.astype(jnp.int32).astype(jnp.float32) * step


def kernel(
    owner_at, slot_at, reads_at, left_at, right_at, frontal_at, inverse_at, ancestor, picked, *scratch
):
    (owner, slot, reads, left, right, frontal, inverse, product, ids, meta_v, meta,
     front, parts, parts_in, solid, x_out, xs_out, x_in, xs_in, mine, z_out, zs_out, z_in, zs_in,
     r_out, rs_out, r_in, rs_in, *rest) = scratch
    sums, rest = rest[:Y], rest[Y:]
    g_all, rest = rest[:CHUNKS], rest[CHUNKS:]
    gs_all, rest = rest[:CHUNKS], rest[CHUNKS:]
    id_sem, x_sem, z_sem, g_sem, r_sem, f_sem, a_sem, own_sem, meta_sem, in_sem = rest

    loads = [
        pltpu.make_async_copy(src, dst, in_sem.at[i])
        for i, (src, dst) in enumerate([
            (left_at, left), (right_at, right), (owner_at, owner), (slot_at, slot),
            (reads_at, reads), (frontal_at, frontal), (inverse_at, inverse),
        ])
    ]
    for copy in loads:
        copy.start()

    pairs, depth, width = left.shape[:3]
    per_dev = frontal.shape[0]
    listed = picked.shape[0]
    part = frontal.shape[2]
    rows = part // CUTS
    count = F * pairs
    around = Y * per_dev
    f = lax.axis_index("forest")
    t = lax.axis_index("tile")
    z, y = t // Y, t % Y

    x_peers = [
        ((f + i) % F, z * Y + (y + l) % Y) for l in range(Y) for i in range(F) if i or l
    ]
    y_peers = [(f, z * Y + (y + i) % Y) for i in range(1, Y)]
    z_peers = [(f, (z + i) % Z * Y + y) for i in range(1, Z)]
    barrier = pltpu.get_barrier_semaphore()
    for peer in x_peers + z_peers:
        pl.semaphore_signal(barrier, inc=1, device_id=peer, device_id_type=MESH)

    def send(src, dst, sems, at, peer):
        copy = pltpu.make_async_remote_copy(
            src_ref=src, dst_ref=dst, send_sem=sems.at[(0,) + at], recv_sem=sems.at[(1,) + at],
            device_id=peer, device_id_type=MESH,
        )
        copy.start()
        return copy

    loads[2].wait()
    loads[3].wait()
    lane = lax.broadcasted_iota(jnp.int32, (8, 128), 1)
    sub = lax.broadcasted_iota(jnp.int32, (8, 128), 0)
    down = jnp.zeros((8, 128), jnp.int32)
    along = jnp.zeros((8, 128), jnp.int32)
    for k in range(pairs):
        group = owner[k] * per_dev + slot[k]
        down = jnp.where(sub == k, group, down)
        along = jnp.where(lane == f * pairs + k, group, along)
    ids[y, f, 0:8, :] = down
    ids[y, f, 8:16, :] = along

    def block_of(ff, yy):
        return yy // 2 * (2 * F) + ff * 2 + yy % 2

    def multiply(col):
        def body(k, carry):
            b = right[k, 0, :, col * HALF:(col + 1) * HALF]
            for tile in range(depth):
                product[col, k, tile * width:(tile + 1) * width] = jnp.dot(
                    left[k, tile], b, preferred_element_type=jnp.float32
                )
            return carry

        lax.fori_loop(0, pairs, body, 0)

    sent = []
    x_copies, z_copies, g_copies, r_copies = {}, {}, {}, {}
    owns = {}

    def start_x(c):
        cut, col = c // 2, c % 2
        if cut == 0:
            multiply(col)

        def pack(b, carry):
            at = pl.multiple_of(b * part + cut * rows, 8)
            v = jnp.concatenate(
                [product[col, k, pl.ds(at, rows)] for k in range(pairs)], axis=0
            )
            x_out[b, c], xs_out[b, c] = encode(v)
            return carry

        lax.fori_loop(0, F * Y, pack, 0, unroll=4)
        if c == 0:
            pl.semaphore_wait(barrier, len(x_peers + z_peers))
        x_copies[c] = []
        for i, peer in enumerate(x_peers):
            b = block_of(peer[0], peer[1] % Y)
            x_copies[c] += [
                send(x_out.at[b, c], x_in.at[y, f, c], x_sem, (0, c, i), peer),
                send(xs_out.at[b, c], xs_in.at[y, f, c], x_sem, (1, c, i), peer),
            ]
        sent.extend(x_copies[c])
        b = block_of(f, y)
        owns[c] = [
            pltpu.make_async_copy(x_out.at[b, c], x_in.at[y, f, c], own_sem.at[0, c]),
            pltpu.make_async_copy(xs_out.at[b, c], xs_in.at[y, f, c], own_sem.at[1, c]),
        ]
        for copy in owns[c]:
            copy.start()

    loads[0].wait()
    loads[1].wait()
    start_x(0)
    id_copies = [
        send(ids.at[y, f], ids.at[y, f], id_sem, (i,), peer) for i, peer in enumerate(x_peers)
    ]
    for copy in loads[4:]:
        copy.wait()
    front_copies = [
        send(frontal.at[:, peer[1] % Y], front.at[y], f_sem, (i,), peer)
        for i, peer in enumerate(y_peers)
    ]
    sent.extend(id_copies + front_copies)
    front[y] = frontal[:, y]
    for c in range(1, CHUNKS):
        start_x(c)

    for copy in id_copies:
        copy.wait_recv()
    number = lax.broadcasted_iota(jnp.int32, (count, 128), 0)
    place = lax.broadcasted_iota(jnp.int32, (count, 128), 1)

    def latest(mask):
        at = jnp.max(jnp.where(mask, number, -1), axis=0, keepdims=True)
        return jnp.broadcast_to(jnp.where(at < 0, count, at), (8, 128))

    for yy in range(Y):
        cols = ids[yy, :, 0:8, :].reshape(count, 128)
        line = jnp.sum(ids[yy, :, 8:16, :], axis=0)
        line = jnp.broadcast_to(line[None], (F, 8, 128)).reshape(count, 128)
        meta_v[yy * 16:yy * 16 + 8, :] = latest((cols == line) & (number < place))
        meta_v[yy * 16 + 8:yy * 16 + 16, :] = latest(cols == place)
        sums[yy][count] = jnp.zeros((rows, HALF), jnp.float32)
    copy = pltpu.make_async_copy(meta_v, meta, meta_sem)
    copy.start()
    copy.wait()

    def start_z(c):
        for copy in x_copies[c]:
            copy.wait_recv()
        for copy in owns[c]:
            copy.wait()

        def chain(ff, carry):
            values = [decode(x_in[yy, ff, c], xs_in[yy, ff, c]) for yy in range(Y)]
            for k in range(pairs):
                j = ff * pairs + k
                for yy in range(Y):
                    earlier = sums[yy][meta[yy * 16, j]]
                    sums[yy][j] = values[yy][k * rows:(k + 1) * rows] + earlier
            return carry

        lax.fori_loop(0, F, chain, 0, unroll=2)

        def pack(zz, carry):
            values = []
            for m in range(around):
                g = zz * around + m
                values.append(sum(sums[yy][meta[yy * 16 + 8, g]] for yy in range(Y)))
            v = jnp.concatenate(values, axis=0)
            mine[c, zz] = v
            z_out[zz, c], zs_out[zz, c] = encode(v)
            return carry

        lax.fori_loop(0, Z, pack, 0, unroll=2)
        z_copies[c] = []
        for i, peer in enumerate(z_peers):
            to = (z + i + 1) % Z
            z_copies[c] += [
                send(z_out.at[to, c], z_in.at[i, c], z_sem, (0, c, i), peer),
                send(zs_out.at[to, c], zs_in.at[i, c], z_sem, (1, c, i), peer),
            ]
        sent.extend(z_copies[c])

    def dot(a, b):
        return jnp.dot(
            a, b, precision=lax.Precision.HIGHEST, preferred_element_type=jnp.float32
        )

    a_copies = []

    def start_g(c):
        cut, col = c // 2, c % 2
        at = slice(cut * rows, (cut + 1) * rows)
        cols = slice(col * HALF, (col + 1) * HALF)
        if c == 0:
            for copy in front_copies:
                copy.wait_recv()
        for copy in z_copies[c]:
            copy.wait_recv()
        v = mine[c, z]
        for i in range(Z - 1):
            v = v + decode(z_in[i, c], zs_in[i, c])
        before = [front[m // per_dev, m % per_dev, at, cols] for m in range(around)]
        v = jnp.concatenate(before, axis=0) - v * (1.0 / depth)
        solid[c] = v
        for m in range(around):
            parts[m // per_dev, m % per_dev, at, cols] = v[m * rows:(m + 1) * rows]
        solved = dot(v, inverse[cols, cols])
        if col:
            solved = solved + dot(solid[c - 1], inverse[0:HALF, cols])
        q, step = encode(solved)
        for m in range(around * rows // 16):
            g_all[c][z, m] = q[m * 16:(m + 1) * 16]
        gs_all[c][z] = step
        g_copies[c] = []
        for i, peer in enumerate(z_peers):
            g_copies[c] += [
                send(g_all[c].at[z], g_all[c].at[z], g_sem, (0, c, i), peer),
                send(gs_all[c].at[z], gs_all[c].at[z], g_sem, (1, c, i), peer),
            ]
        sent.extend(g_copies[c])
        if c == CHUNKS - 1:
            for i, peer in enumerate(y_peers):
                a_copies.append(
                    send(parts.at[peer[1] % Y], parts_in.at[y], a_sem, (i,), peer)
                )
            sent.extend(a_copies)
            parts_in[y] = parts[y]

    def start_r(c):
        for copy in g_copies[c]:
            copy.wait_recv()
        r_copies[c] = []
        for i in range(Y):
            to = (y + i) % Y
            values = []
            for r in range(listed):
                g = reads[(z * Y + to) * listed + r]
                at = g % around
                if rows == 16:
                    q = g_all[c][g // around, at].astype(jnp.int32)
                else:
                    q = g_all[c][g // around, at // 2].astype(jnp.int32)
                    q = jnp.where(at % 2 == 1, q[8:16], q[0:8])
                values.append(q)
            q = jnp.concatenate(values, axis=0).astype(jnp.int16)
            for r in range(listed):
                g = reads[(z * Y + to) * listed + r]
                step = gs_all[c][g // around]
                if i == 0:
                    rs_in[y, c, r] = step
                else:
                    rs_out[i - 1, c, r] = step
            if i == 0:
                r_in[y, c] = q
                continue
            r_out[i - 1, c] = q
            peer = y_peers[i - 1]
            r_copies[c] += [
                send(r_out.at[i - 1, c], r_in.at[y, c], r_sem, (0, c, i - 1), peer),
                send(rs_out.at[i - 1, c], rs_in.at[y, c], r_sem, (1, c, i - 1), peer),
            ]
        sent.extend(r_copies[c])

    def finish(c):
        cut, col = c // 2, c % 2
        for copy in r_copies[c]:
            copy.wait_recv()
        for yy in range(Y):
            q = r_in[yy, c].astype(jnp.int32).astype(jnp.float32)
            for r in range(listed):
                picked[r, yy, cut * rows:(cut + 1) * rows, col * HALF:(col + 1) * HALF] = (
                    q[r * rows:(r + 1) * rows] * rs_in[yy, c, r]
                )

    stages = (start_z, start_g, start_r, finish)
    for wave in range(CHUNKS + len(stages) - 1):
        for number_of, stage in reversed(list(enumerate(stages))):
            if 0 <= wave - number_of < CHUNKS:
                stage(wave - number_of)

    for copy in a_copies:
        copy.wait_recv()
    for yy in range(Y):
        for s in range(per_dev):
            ancestor[s, yy] = parts_in[yy, s]
    for copy in sent:
        copy.wait_send()


def per_device(
    left_panels, right_panels, dest_owner, tile_slot, frontal_tiles, diag_inverse, reader_tile
):
    left = left_panels[0]
    right = right_panels[0]
    pairs, depth, width = left.shape[:3]
    per_dev = frontal_tiles.shape[0]
    listed = reader_tile.shape[0] // lax.axis_size("tile")
    part = depth * (width // F) // Y
    rows = part // CUTS
    count = F * pairs
    around = Y * per_dev
    frontal = frontal_tiles.reshape(per_dev, Y, part, width)
    n = CHUNKS

    def f32(*shape):
        return pltpu.VMEM(shape, jnp.float32)

    def i16(*shape):
        return pltpu.VMEM(shape, jnp.int16)

    dma = pltpu.SemaphoreType.DMA
    scratch = [
        pltpu.SMEM((pairs,), jnp.int32),
        pltpu.SMEM((pairs,), jnp.int32),
        pltpu.SMEM(reader_tile.shape, jnp.int32),
        pltpu.VMEM(left.shape, left.dtype),
        pltpu.VMEM(right.shape, right.dtype),
        f32(*frontal.shape),
        f32(*diag_inverse.shape),
        f32(2, pairs, depth * width, HALF),
        pltpu.VMEM((Y, F, 16, 128), jnp.int32),
        pltpu.VMEM((Y * 16, 128), jnp.int32),
        pltpu.SMEM((Y * 16, 128), jnp.int32),
        f32(Y, per_dev, part, width),
        f32(Y, per_dev, part, width),
        f32(Y, per_dev, part, width),
        f32(n, around * rows, HALF),
        i16(F * Y, n, pairs * rows, HALF),
        f32(F * Y, n, 1, HALF),
        i16(Y, F, n, pairs * rows, HALF),
        f32(Y, F, n, 1, HALF),
        f32(n, Z, around * rows, HALF),
        i16(Z, n, around * rows, HALF),
        f32(Z, n, 1, HALF),
        i16(Z - 1, n, around * rows, HALF),
        f32(Z - 1, n, 1, HALF),
        i16(Y - 1, n, listed * rows, HALF),
        f32(Y - 1, n, listed, 1, HALF),
        i16(Y, n, listed * rows, HALF),
        f32(Y, n, listed, 1, HALF),
        *[f32(count + 1, rows, HALF)] * Y,
        *[i16(Z, around * rows // 16, 16, HALF)] * n,
        *[f32(Z, 1, HALF)] * n,
        dma((2, F * Y - 1)),
        dma((2, 2, n, F * Y - 1)),
        dma((2, 2, n, Z - 1)),
        dma((2, 2, n, Z - 1)),
        dma((2, 2, n, Y - 1)),
        dma((2, Y - 1)),
        dma((2, Y - 1)),
        dma((2, n)),
        dma,
        dma((7,)),
    ]
    any_place = pl.BlockSpec(memory_space=pl.ANY)
    vmem = pl.BlockSpec(memory_space=pltpu.VMEM)
    ancestor, picked = pl.pallas_call(
        kernel,
        out_shape=(
            jax.ShapeDtypeStruct(frontal.shape, jnp.float32),
            jax.ShapeDtypeStruct((listed,) + frontal.shape[1:], jnp.float32),
        ),
        in_specs=[any_place] * 7,
        out_specs=(vmem, vmem),
        scratch_shapes=scratch,
        compiler_params=pltpu.CompilerParams(
            collective_id=0, has_side_effects=True, vmem_limit_bytes=60 << 20
        ),
        cost_estimate=pl.CostEstimate(
            flops=2 * pairs * depth * width**3, bytes_accessed=4 << 20, transcendentals=0
        ),
        name="schur_update",
    )(dest_owner[0, :, 0], tile_slot[0], reader_tile, left, right, frontal, diag_inverse)
    return (
        ancestor.reshape(frontal_tiles.shape),
        picked.reshape((listed,) + frontal_tiles.shape[1:]),
    )


def solution(mesh):
    placed = (
        P("forest", "tile", None, None, None),
        P("forest", "tile", None, None, None),
        P("forest", "tile", None),
        P("forest", "tile"),
        P("tile", None, "forest", None),
        P(),
        P(),
    )
    return jax.shard_map(
        per_device,
        mesh=mesh,
        in_specs=placed,
        out_specs=(P("tile", None, "forest", None), P("tile", None, "forest", None)),
        check_vma=False,
    )
```

```python
import functools

import jax
import jax.numpy as jnp
from jax import lax
from jax.experimental import pallas as pl
from jax.experimental.pallas import tpu as pltpu
from jax.sharding import PartitionSpec as P

MESH = pl.DeviceIdType.MESH
Y = 4
Z = 8
F = 8
HALF = 128
CUTS = 1
CHUNKS = 2 * CUTS
TOP = 32767.0


def scale_of(v):
    v = jnp.abs(v)
    most = functools.reduce(jnp.maximum, [v[i:i + 8] for i in range(0, v.shape[0], 8)])
    most = jnp.maximum(jnp.max(most, axis=0, keepdims=True), 1e-30)
    return most * (1.0 / TOP), TOP / most


def encode(v):
    step, back = scale_of(v)
    return jnp.round(v * back).astype(jnp.int32).astype(jnp.int16), step


def decode(q, step):
    return q.astype(jnp.int32).astype(jnp.float32) * step


def kernel(
    owner_at, slot_at, reads_at, left_at, right_at, frontal_at, inverse_at, ancestor, picked, *scratch
):
    (owner, slot, reads, left, right, frontal, inverse, product, ids, meta_v, meta,
     front, parts, parts_in, solid, x_out, xs_out, x_in, xs_in, mine, z_out, zs_out, z_in, zs_in,
     r_out, rs_out, r_in, rs_in, *rest) = scratch
    sums, rest = rest[:Y], rest[Y:]
    g_all, rest = rest[:CHUNKS], rest[CHUNKS:]
    gs_all, rest = rest[:CHUNKS], rest[CHUNKS:]
    id_sem, x_sem, z_sem, g_sem, r_sem, f_sem, a_sem, own_sem, meta_sem, in_sem = rest

    loads = [
        pltpu.make_async_copy(src, dst, in_sem.at[i])
        for i, (src, dst) in enumerate([
            (left_at, left), (right_at, right), (owner_at, owner), (slot_at, slot),
            (reads_at, reads), (frontal_at, frontal), (inverse_at, inverse),
        ])
    ]
    for copy in loads:
        copy.start()

    pairs, depth, width = left.shape[:3]
    per_dev = frontal.shape[0]
    listed = picked.shape[0]
    part = frontal.shape[2]
    rows = part // CUTS
    count = F * pairs
    around = Y * per_dev
    f = lax.axis_index("forest")
    t = lax.axis_index("tile")
    z, y = t // Y, t % Y

    x_peers = [
        ((f + i) % F, z * Y + (y + l) % Y) for l in range(Y) for i in range(F) if i or l
    ]
    y_peers = [(f, z * Y + (y + i) % Y) for i in range(1, Y)]
    z_peers = [(f, (z + i) % Z * Y + y) for i in range(1, Z)]
    barrier = pltpu.get_barrier_semaphore()
    for peer in x_peers + z_peers:
        pl.semaphore_signal(barrier, inc=1, device_id=peer, device_id_type=MESH)

    def send(src, dst, sems, at, peer):
        pltpu.make_async_remote_copy(
            src_ref=src, dst_ref=dst, send_sem=sems.at[(0,) + at], recv_sem=sems.at[(1,) + at],
            device_id=peer, device_id_type=MESH,
        ).start()

    def wait(way, like, sems, at):
        pltpu.make_async_copy(like, like, sems.at[(way,) + at]).wait()

    loads[2].wait()
    loads[3].wait()
    lane = lax.broadcasted_iota(jnp.int32, (8, 128), 1)
    sub = lax.broadcasted_iota(jnp.int32, (8, 128), 0)
    down = jnp.zeros((8, 128), jnp.int32)
    along = jnp.zeros((8, 128), jnp.int32)
    for k in range(pairs):
        group = owner[k] * per_dev + slot[k]
        down = jnp.where(sub == k, group, down)
        along = jnp.where(lane == f * pairs + k, group, along)
    ids[y * F + f, 0:8, :] = down
    ids[y * F + f, 8:16, :] = along

    def block_of(ff, yy):
        return yy // 2 * (2 * F) + ff * 2 + yy % 2

    def multiply(col):
        def body(k, carry):
            b = right[k, 0, :, col * HALF:(col + 1) * HALF]
            for tile in range(depth):
                product[col, k, tile * width:(tile + 1) * width] = jnp.dot(
                    left[k, tile], b, preferred_element_type=jnp.float32
                )
            return carry

        lax.fori_loop(0, pairs, body, 0)

    last = F * Y - 1
    owns = {}

    def start_x(c):
        cut, col = c // 2, c % 2
        if cut == 0:
            multiply(col)

        def pack(b, carry):
            at = pl.multiple_of(b * part + cut * rows, 8)
            v = jnp.concatenate(
                [product[col, k, pl.ds(at, rows)] for k in range(pairs)], axis=0
            )
            x_out[b, c], xs_out[b, c] = encode(v)
            return carry

        lax.fori_loop(0, F * Y, pack, 0, unroll=4)
        if c == 0:
            pl.semaphore_wait(barrier, len(x_peers + z_peers))
        for peer in x_peers:
            b = block_of(peer[0], peer[1] % Y)
            send(x_out.at[b, c], x_in.at[y * F + f, c], x_sem, (0, c), peer)
            send(xs_out.at[b, c], xs_in.at[y * F + f, c], x_sem, (1, c), peer)
        b = block_of(f, y)
        owns[c] = [
            pltpu.make_async_copy(x_out.at[b, c], x_in.at[y * F + f, c], own_sem.at[0, c]),
            pltpu.make_async_copy(xs_out.at[b, c], xs_in.at[y * F + f, c], own_sem.at[1, c]),
        ]
        for copy in owns[c]:
            copy.start()

    loads[0].wait()
    loads[1].wait()
    start_x(0)
    for peer in x_peers:
        send(ids.at[y * F + f], ids.at[y * F + f], id_sem, (), peer)
    for copy in loads[4:]:
        copy.wait()
    for peer in y_peers:
        send(frontal.at[:, peer[1] % Y], front.at[y], f_sem, (), peer)
    front[y] = frontal[:, y]
    for c in range(1, CHUNKS):
        start_x(c)

    wait(1, ids.at[pl.ds(0, last)], id_sem, ())
    number = lax.broadcasted_iota(jnp.int32, (count, 128), 0)
    place = lax.broadcasted_iota(jnp.int32, (count, 128), 1)

    def latest(mask):
        at = jnp.max(jnp.where(mask, number, -1), axis=0, keepdims=True)
        return jnp.broadcast_to(jnp.where(at < 0, count, at), (8, 128))

    for yy in range(Y):
        cols = ids[yy * F:(yy + 1) * F, 0:8, :].reshape(count, 128)
        line = jnp.sum(ids[yy * F:(yy + 1) * F, 8:16, :], axis=0)
        line = jnp.broadcast_to(line[None], (F, 8, 128)).reshape(count, 128)
        meta_v[yy * 16:yy * 16 + 8, :] = latest((cols == line) & (number < place))
        meta_v[yy * 16 + 8:yy * 16 + 16, :] = latest(cols == place)
        sums[yy][count] = jnp.zeros((rows, HALF), jnp.float32)
    copy = pltpu.make_async_copy(meta_v, meta, meta_sem)
    copy.start()
    copy.wait()

    def start_z(c):
        wait(1, x_in.at[pl.ds(0, last), c], x_sem, (0, c))
        wait(1, xs_in.at[pl.ds(0, last), c], x_sem, (1, c))
        for copy in owns[c]:
            copy.wait()

        def chain(ff, carry):
            values = [decode(x_in[yy * F + ff, c], xs_in[yy * F + ff, c]) for yy in range(Y)]
            for k in range(pairs):
                j = ff * pairs + k
                for yy in range(Y):
                    earlier = sums[yy][meta[yy * 16, j]]
                    sums[yy][j] = values[yy][k * rows:(k + 1) * rows] + earlier
            return carry

        lax.fori_loop(0, F, chain, 0, unroll=2)

        def pack(zz, carry):
            values = []
            for m in range(around):
                g = zz * around + m
                values.append(sum(sums[yy][meta[yy * 16 + 8, g]] for yy in range(Y)))
            v = jnp.concatenate(values, axis=0)
            mine[c, zz] = v
            z_out[zz, c], zs_out[zz, c] = encode(v)
            return carry

        lax.fori_loop(0, Z, pack, 0, unroll=2)
        for i, peer in enumerate(z_peers):
            to = (z + i + 1) % Z
            send(z_out.at[to, c], z_in.at[i, c], z_sem, (0, c), peer)
            send(zs_out.at[to, c], zs_in.at[i, c], z_sem, (1, c), peer)

    def dot(a, b):
        return jnp.dot(
            a, b, precision=lax.Precision.HIGHEST, preferred_element_type=jnp.float32
        )

    def start_g(c):
        cut, col = c // 2, c % 2
        at = slice(cut * rows, (cut + 1) * rows)
        cols = slice(col * HALF, (col + 1) * HALF)
        if c == 0:
            wait(1, front.at[pl.ds(0, Y - 1)], f_sem, ())
        wait(1, z_in.at[:, c], z_sem, (0, c))
        wait(1, zs_in.at[:, c], z_sem, (1, c))
        v = mine[c, z]
        for i in range(Z - 1):
            v = v + decode(z_in[i, c], zs_in[i, c])
        before = [front[m // per_dev, m % per_dev, at, cols] for m in range(around)]
        v = jnp.concatenate(before, axis=0) - v * (1.0 / depth)
        solid[c] = v
        for m in range(around):
            parts[m // per_dev, m % per_dev, at, cols] = v[m * rows:(m + 1) * rows]
        solved = dot(v, inverse[cols, cols])
        if col:
            solved = solved + dot(solid[c - 1], inverse[0:HALF, cols])
        q, step = encode(solved)
        for m in range(around * rows // 16):
            g_all[c][z, m] = q[m * 16:(m + 1) * 16]
        gs_all[c][z] = step
        for peer in z_peers:
            send(g_all[c].at[z], g_all[c].at[z], g_sem, (0, c), peer)
            send(gs_all[c].at[z], gs_all[c].at[z], g_sem, (1, c), peer)
        if c == CHUNKS - 1:
            for peer in y_peers:
                send(parts.at[peer[1] % Y], parts_in.at[y], a_sem, (), peer)
            parts_in[y] = parts[y]

    def start_r(c):
        wait(1, g_all[c].at[pl.ds(0, Z - 1)], g_sem, (0, c))
        wait(1, gs_all[c].at[pl.ds(0, Z - 1)], g_sem, (1, c))
        for i in range(Y):
            to = (y + i) % Y
            values = []
            for r in range(listed):
                g = reads[(z * Y + to) * listed + r]
                at = g % around
                if rows == 16:
                    q = g_all[c][g // around, at].astype(jnp.int32)
                else:
                    q = g_all[c][g // around, at // 2].astype(jnp.int32)
                    q = jnp.where(at % 2 == 1, q[8:16], q[0:8])
                values.append(q)
            q = jnp.concatenate(values, axis=0).astype(jnp.int16)
            for r in range(listed):
                g = reads[(z * Y + to) * listed + r]
                step = gs_all[c][g // around]
                if i == 0:
                    rs_in[y, c, r] = step
                else:
                    rs_out[i - 1, c, r] = step
            if i == 0:
                r_in[y, c] = q
                continue
            r_out[i - 1, c] = q
            peer = y_peers[i - 1]
            send(r_out.at[i - 1, c], r_in.at[y, c], r_sem, (0, c), peer)
            send(rs_out.at[i - 1, c], rs_in.at[y, c], r_sem, (1, c), peer)

    def finish(c):
        cut, col = c // 2, c % 2
        wait(1, r_in.at[pl.ds(0, Y - 1), c], r_sem, (0, c))
        wait(1, rs_in.at[pl.ds(0, Y - 1), c], r_sem, (1, c))
        for yy in range(Y):
            q = r_in[yy, c].astype(jnp.int32).astype(jnp.float32)
            for r in range(listed):
                picked[r, yy, cut * rows:(cut + 1) * rows, col * HALF:(col + 1) * HALF] = (
                    q[r * rows:(r + 1) * rows] * rs_in[yy, c, r]
                )

    stages = (start_z, start_g, start_r, finish)
    for wave in range(CHUNKS + len(stages) - 1):
        for number_of, stage in reversed(list(enumerate(stages))):
            if 0 <= wave - number_of < CHUNKS:
                stage(wave - number_of)

    wait(1, parts_in.at[pl.ds(0, Y - 1)], a_sem, ())
    for yy in range(Y):
        for s in range(per_dev):
            ancestor[s, yy] = parts_in[yy, s]
    wait(0, ids.at[pl.ds(0, last)], id_sem, ())
    wait(0, front.at[pl.ds(0, Y - 1)], f_sem, ())
    wait(0, parts.at[pl.ds(0, Y - 1)], a_sem, ())
    for c in range(CHUNKS):
        wait(0, x_out.at[pl.ds(0, last), c], x_sem, (0, c))
        wait(0, xs_out.at[pl.ds(0, last), c], x_sem, (1, c))
        wait(0, z_out.at[pl.ds(0, Z - 1), c], z_sem, (0, c))
        wait(0, zs_out.at[pl.ds(0, Z - 1), c], z_sem, (1, c))
        wait(0, g_all[c].at[pl.ds(0, Z - 1)], g_sem, (0, c))
        wait(0, gs_all[c].at[pl.ds(0, Z - 1)], g_sem, (1, c))
        wait(0, r_out.at[:, c], r_sem, (0, c))
        wait(0, rs_out.at[:, c], r_sem, (1, c))


def per_device(
    left_panels, right_panels, dest_owner, tile_slot, frontal_tiles, diag_inverse, reader_tile
):
    left = left_panels[0]
    right = right_panels[0]
    pairs, depth, width = left.shape[:3]
    per_dev = frontal_tiles.shape[0]
    listed = reader_tile.shape[0] // lax.axis_size("tile")
    part = depth * (width // F) // Y
    rows = part // CUTS
    count = F * pairs
    around = Y * per_dev
    frontal = frontal_tiles.reshape(per_dev, Y, part, width)
    n = CHUNKS

    def f32(*shape):
        return pltpu.VMEM(shape, jnp.float32)

    def i16(*shape):
        return pltpu.VMEM(shape, jnp.int16)

    dma = pltpu.SemaphoreType.DMA
    scratch = [
        pltpu.SMEM((pairs,), jnp.int32),
        pltpu.SMEM((pairs,), jnp.int32),
        pltpu.SMEM(reader_tile.shape, jnp.int32),
        pltpu.VMEM(left.shape, left.dtype),
        pltpu.VMEM(right.shape, right.dtype),
        f32(*frontal.shape),
        f32(*diag_inverse.shape),
        f32(2, pairs, depth * width, HALF),
        pltpu.VMEM((Y * F, 16, 128), jnp.int32),
        pltpu.VMEM((Y * 16, 128), jnp.int32),
        pltpu.SMEM((Y * 16, 128), jnp.int32),
        f32(Y, per_dev, part, width),
        f32(Y, per_dev, part, width),
        f32(Y, per_dev, part, width),
        f32(n, around * rows, HALF),
        i16(F * Y, n, pairs * rows, HALF),
        f32(F * Y, n, 1, HALF),
        i16(Y * F, n, pairs * rows, HALF),
        f32(Y * F, n, 1, HALF),
        f32(n, Z, around * rows, HALF),
        i16(Z, n, around * rows, HALF),
        f32(Z, n, 1, HALF),
        i16(Z - 1, n, around * rows, HALF),
        f32(Z - 1, n, 1, HALF),
        i16(Y - 1, n, listed * rows, HALF),
        f32(Y - 1, n, listed, 1, HALF),
        i16(Y, n, listed * rows, HALF),
        f32(Y, n, listed, 1, HALF),
        *[f32(count + 1, rows, HALF)] * Y,
        *[i16(Z, around * rows // 16, 16, HALF)] * n,
        *[f32(Z, 1, HALF)] * n,
        dma((2,)),
        dma((2, 2, n)),
        dma((2, 2, n)),
        dma((2, 2, n)),
        dma((2, 2, n)),
        dma((2,)),
        dma((2,)),
        dma((2, n)),
        dma,
        dma((7,)),
    ]
    hbm = pl.BlockSpec(memory_space=pltpu.HBM)
    vmem = pl.BlockSpec(memory_space=pltpu.VMEM)
    ancestor, picked = pl.pallas_call(
        kernel,
        out_shape=(
            jax.ShapeDtypeStruct(frontal.shape, jnp.float32),
            jax.ShapeDtypeStruct((listed,) + frontal.shape[1:], jnp.float32),
        ),
        in_specs=[hbm] * 7,
        out_specs=(vmem, vmem),
        scratch_shapes=scratch,
        compiler_params=pltpu.CompilerParams(
            collective_id=0, has_side_effects=True, vmem_limit_bytes=60 << 20
        ),
        cost_estimate=pl.CostEstimate(
            flops=2 * pairs * depth * width**3, bytes_accessed=4 << 20, transcendentals=0
        ),
        name="schur_update",
    )(dest_owner[0, :, 0], tile_slot[0], reader_tile, left, right, frontal, diag_inverse)
    return (
        ancestor.reshape(frontal_tiles.shape),
        picked.reshape((listed,) + frontal_tiles.shape[1:]),
    )


def solution(mesh):
    placed = (
        P("forest", "tile", None, None, None),
        P("forest", "tile", None, None, None),
        P("forest", "tile", None),
        P("forest", "tile"),
        P("tile", None, "forest", None),
        P(),
        P(),
    )
    return jax.shard_map(
        per_device,
        mesh=mesh,
        in_specs=placed,
        out_specs=(P("tile", None, "forest", None), P("tile", None, "forest", None)),
        check_vma=False,
    )
```

```python
import functools

import jax
import jax.numpy as jnp
from jax import lax
from jax.experimental import pallas as pl
from jax.experimental.pallas import tpu as pltpu
from jax.sharding import PartitionSpec as P

MESH = pl.DeviceIdType.MESH
Y = 4
Z = 8
F = 8
HALF = 128
CUTS = 1
CHUNKS = 2 * CUTS
TOP = 32767.0


def scale_of(v):
    v = jnp.abs(v)
    most = functools.reduce(jnp.maximum, [v[i:i + 8] for i in range(0, v.shape[0], 8)])
    most = jnp.maximum(jnp.max(most, axis=0, keepdims=True), 1e-30)
    return most * (1.0 / TOP), TOP / most


def encode(v):
    step, back = scale_of(v)
    return jnp.round(v * back).astype(jnp.int32).astype(jnp.int16), step


def decode(q, step):
    return q.astype(jnp.int32).astype(jnp.float32) * step


def kernel(
    owner_at, slot_at, reads_at, left_at, right_at, frontal_at, inverse_at, ancestor, picked, *scratch
):
    (owner, slot, reads, left, right, frontal, inverse, product, ids, meta_v, meta,
     front, parts, parts_in, solid, x_out, xs_out, x_in, xs_in, mine, z_out, zs_out, z_in, zs_in,
     r_out, rs_out, r_in, rs_in, *rest) = scratch
    sums, rest = rest[:Y], rest[Y:]
    g_all, rest = rest[:CHUNKS], rest[CHUNKS:]
    gs_all, rest = rest[:CHUNKS], rest[CHUNKS:]
    id_sem, x_sem, z_sem, g_sem, r_sem, f_sem, a_sem, own_sem, meta_sem, in_sem = rest

    loads = [
        pltpu.make_async_copy(src, dst, in_sem.at[i])
        for i, (src, dst) in enumerate([
            (left_at, left), (right_at, right), (owner_at, owner), (slot_at, slot),
            (reads_at, reads), (frontal_at, frontal), (inverse_at, inverse),
        ])
    ]
    for copy in loads:
        copy.start()

    pairs, depth, width = left.shape[:3]
    per_dev = frontal.shape[0]
    listed = picked.shape[0]
    part = frontal.shape[2]
    rows = part // CUTS
    count = F * pairs
    around = Y * per_dev
    f = lax.axis_index("forest")
    t = lax.axis_index("tile")
    z, y = t // Y, t % Y

    x_peers = [
        ((f + i) % F, z * Y + (y + l) % Y) for l in range(Y) for i in range(F) if i or l
    ]
    y_peers = [(f, z * Y + (y + i) % Y) for i in range(1, Y)]
    z_peers = [(f, (z + i) % Z * Y + y) for i in range(1, Z)]
    barrier = pltpu.get_barrier_semaphore()
    for peer in x_peers + z_peers:
        pl.semaphore_signal(barrier, inc=1, device_id=peer, device_id_type=MESH)

    def send(src, dst, sems, at, peer):
        pltpu.make_async_remote_copy(
            src_ref=src, dst_ref=dst, send_sem=sems.at[(0,) + at], recv_sem=sems.at[(1,) + at],
            device_id=peer, device_id_type=MESH,
        ).start()

    def wait(way, like, sems, at):
        pltpu.make_async_copy(like, like, sems.at[(way,) + at]).wait()

    loads[2].wait()
    loads[3].wait()
    lane = lax.broadcasted_iota(jnp.int32, (8, 128), 1)
    sub = lax.broadcasted_iota(jnp.int32, (8, 128), 0)
    down = jnp.zeros((8, 128), jnp.int32)
    along = jnp.zeros((8, 128), jnp.int32)
    for k in range(pairs):
        group = owner[k] * per_dev + slot[k]
        down = jnp.where(sub == k, group, down)
        along = jnp.where(lane == f * pairs + k, group, along)
    ids[y * F + f, 0:8, :] = down
    ids[y * F + f, 8:16, :] = along

    def block_of(ff, yy):
        return yy // 2 * (2 * F) + ff * 2 + yy % 2

    def multiply(col):
        def body(k, carry):
            b = right[k, 0, :, col * HALF:(col + 1) * HALF]
            for tile in range(depth):
                product[col, k, tile * width:(tile + 1) * width] = jnp.dot(
                    left[k, tile], b, preferred_element_type=jnp.float32
                )
            return carry

        lax.fori_loop(0, pairs, body, 0)

    last = F * Y - 1
    owns = {}

    def start_x(c):
        cut, col = c // 2, c % 2
        if cut == 0:
            multiply(col)

        def pack(b, carry):
            at = pl.multiple_of(b * part + cut * rows, 8)
            v = jnp.concatenate(
                [product[col, k, pl.ds(at, rows)] for k in range(pairs)], axis=0
            )
            x_out[b, c], xs_out[b, c] = encode(v)
            return carry

        lax.fori_loop(0, F * Y, pack, 0, unroll=4)
        if c == 0:
            pl.semaphore_wait(barrier, len(x_peers + z_peers))
        for peer in x_peers:
            b = block_of(peer[0], peer[1] % Y)
            send(x_out.at[b, c], x_in.at[y * F + f, c], x_sem, (0, c), peer)
            send(xs_out.at[b, c], xs_in.at[y * F + f, c], x_sem, (1, c), peer)
        b = block_of(f, y)
        owns[c] = [
            pltpu.make_async_copy(x_out.at[b, c], x_in.at[y * F + f, c], own_sem.at[0, c]),
            pltpu.make_async_copy(xs_out.at[b, c], xs_in.at[y * F + f, c], own_sem.at[1, c]),
        ]
        for copy in owns[c]:
            copy.start()

    loads[0].wait()
    loads[1].wait()
    start_x(0)
    for peer in x_peers:
        send(ids.at[y * F + f], ids.at[y * F + f], id_sem, (), peer)
    for copy in loads[4:]:
        copy.wait()
    for peer in y_peers:
        send(frontal.at[:, peer[1] % Y], front.at[y], f_sem, (), peer)
    front[y] = frontal[:, y]
    for c in range(1, CHUNKS):
        start_x(c)

    wait(1, ids.at[pl.ds(0, last)], id_sem, ())
    number = lax.broadcasted_iota(jnp.int32, (count, 128), 0)
    place = lax.broadcasted_iota(jnp.int32, (count, 128), 1)

    def latest(mask):
        at = jnp.max(jnp.where(mask, number, -1), axis=0, keepdims=True)
        return jnp.broadcast_to(jnp.where(at < 0, count, at), (8, 128))

    for yy in range(Y):
        cols = ids[yy * F:(yy + 1) * F, 0:8, :].reshape(count, 128)
        line = jnp.sum(ids[yy * F:(yy + 1) * F, 8:16, :], axis=0)
        line = jnp.broadcast_to(line[None], (F, 8, 128)).reshape(count, 128)
        meta_v[yy * 16:yy * 16 + 8, :] = latest((cols == line) & (number < place))
        meta_v[yy * 16 + 8:yy * 16 + 16, :] = latest(cols == place)
        sums[yy][count] = jnp.zeros((rows, HALF), jnp.float32)
    copy = pltpu.make_async_copy(meta_v, meta, meta_sem)
    copy.start()
    copy.wait()

    def start_z(c):
        wait(1, x_in.at[pl.ds(0, last), c], x_sem, (0, c))
        wait(1, xs_in.at[pl.ds(0, last), c], x_sem, (1, c))
        for copy in owns[c]:
            copy.wait()

        def chain(ff, carry):
            values = [decode(x_in[yy * F + ff, c], xs_in[yy * F + ff, c]) for yy in range(Y)]
            for k in range(pairs):
                j = ff * pairs + k
                for yy in range(Y):
                    earlier = sums[yy][meta[yy * 16, j]]
                    sums[yy][j] = values[yy][k * rows:(k + 1) * rows] + earlier
            return carry

        lax.fori_loop(0, F, chain, 0, unroll=2)

        def pack(zz, carry):
            values = []
            for m in range(around):
                g = zz * around + m
                values.append(sum(sums[yy][meta[yy * 16 + 8, g]] for yy in range(Y)))
            v = jnp.concatenate(values, axis=0)
            mine[c, zz] = v
            z_out[zz, c], zs_out[zz, c] = encode(v)
            return carry

        lax.fori_loop(0, Z, pack, 0, unroll=2)
        for i, peer in enumerate(z_peers):
            to = (z + i + 1) % Z
            send(z_out.at[to, c], z_in.at[i, c], z_sem, (0, c), peer)
            send(zs_out.at[to, c], zs_in.at[i, c], z_sem, (1, c), peer)

    def dot(a, b):
        return jnp.dot(
            a, b, precision=lax.Precision.HIGHEST, preferred_element_type=jnp.float32
        )

    def start_g(c):
        cut, col = c // 2, c % 2
        at = slice(cut * rows, (cut + 1) * rows)
        cols = slice(col * HALF, (col + 1) * HALF)
        if c == 0:
            wait(1, front.at[pl.ds(0, Y - 1)], f_sem, ())
        wait(1, z_in.at[:, c], z_sem, (0, c))
        wait(1, zs_in.at[:, c], z_sem, (1, c))
        v = mine[c, z]
        for i in range(Z - 1):
            v = v + decode(z_in[i, c], zs_in[i, c])
        before = [front[m // per_dev, m % per_dev, at, cols] for m in range(around)]
        v = jnp.concatenate(before, axis=0) - v * (1.0 / depth)
        solid[c] = v
        for m in range(around):
            parts[m // per_dev, m % per_dev, at, cols] = v[m * rows:(m + 1) * rows]
        solved = dot(v, inverse[cols, cols])
        if col:
            solved = solved + dot(solid[c - 1], inverse[0:HALF, cols])
        q, step = encode(solved)
        for m in range(around * rows // 16):
            g_all[c][z, m] = q[m * 16:(m + 1) * 16]
        gs_all[c][z] = step
        for peer in z_peers:
            send(g_all[c].at[z], g_all[c].at[z], g_sem, (0, c), peer)
            send(gs_all[c].at[z], gs_all[c].at[z], g_sem, (1, c), peer)
        if c == CHUNKS - 1:
            for peer in y_peers:
                send(parts.at[peer[1] % Y], parts_in.at[y], a_sem, (), peer)
            parts_in[y] = parts[y]

    def start_r(c):
        wait(1, g_all[c].at[pl.ds(0, Z - 1)], g_sem, (0, c))
        wait(1, gs_all[c].at[pl.ds(0, Z - 1)], g_sem, (1, c))
        for i in range(Y):
            to = (y + i) % Y
            values = []
            for r in range(listed):
                g = reads[(z * Y + to) * listed + r]
                at = g % around
                if rows == 16:
                    q = g_all[c][g // around, at].astype(jnp.int32)
                else:
                    q = g_all[c][g // around, at // 2].astype(jnp.int32)
                    q = jnp.where(at % 2 == 1, q[8:16], q[0:8])
                values.append(q)
            q = jnp.concatenate(values, axis=0).astype(jnp.int16)
            for r in range(listed):
                g = reads[(z * Y + to) * listed + r]
                step = gs_all[c][g // around]
                if i == 0:
                    rs_in[y, c, r] = step
                else:
                    rs_out[i - 1, c, r] = step
            if i == 0:
                r_in[y, c] = q
                continue
            r_out[i - 1, c] = q
            peer = y_peers[i - 1]
            send(r_out.at[i - 1, c], r_in.at[y, c], r_sem, (0, c), peer)
            send(rs_out.at[i - 1, c], rs_in.at[y, c], r_sem, (1, c), peer)

    def finish(c):
        cut, col = c // 2, c % 2
        wait(1, r_in.at[pl.ds(0, Y - 1), c], r_sem, (0, c))
        wait(1, rs_in.at[pl.ds(0, Y - 1), c], r_sem, (1, c))
        for yy in range(Y):
            q = r_in[yy, c].astype(jnp.int32).astype(jnp.float32)
            for r in range(listed):
                picked[r, yy, cut * rows:(cut + 1) * rows, col * HALF:(col + 1) * HALF] = (
                    q[r * rows:(r + 1) * rows] * rs_in[yy, c, r]
                )

    stages = (start_z, start_g, start_r, finish)
    for wave in range(CHUNKS + len(stages) - 1):
        for number_of, stage in reversed(list(enumerate(stages))):
            if 0 <= wave - number_of < CHUNKS:
                stage(wave - number_of)

    wait(1, parts_in.at[pl.ds(0, Y - 1)], a_sem, ())
    for yy in range(Y):
        for s in range(per_dev):
            ancestor[s, yy] = parts_in[yy, s]
    wait(0, ids.at[pl.ds(0, last)], id_sem, ())
    wait(0, front.at[pl.ds(0, Y - 1)], f_sem, ())
    wait(0, parts.at[pl.ds(0, Y - 1)], a_sem, ())
    for c in range(CHUNKS):
        wait(0, x_out.at[pl.ds(0, last), c], x_sem, (0, c))
        wait(0, xs_out.at[pl.ds(0, last), c], x_sem, (1, c))
        wait(0, z_out.at[pl.ds(0, Z - 1), c], z_sem, (0, c))
        wait(0, zs_out.at[pl.ds(0, Z - 1), c], z_sem, (1, c))
        wait(0, g_all[c].at[pl.ds(0, Z - 1)], g_sem, (0, c))
        wait(0, gs_all[c].at[pl.ds(0, Z - 1)], g_sem, (1, c))
        wait(0, r_out.at[:, c], r_sem, (0, c))
        wait(0, rs_out.at[:, c], r_sem, (1, c))


def per_device(
    left_panels, right_panels, dest_owner, tile_slot, frontal_tiles, diag_inverse, reader_tile
):
    left = left_panels[0]
    right = right_panels[0]
    pairs, depth, width = left.shape[:3]
    per_dev = frontal_tiles.shape[0]
    listed = reader_tile.shape[0] // lax.axis_size("tile")
    part = depth * (width // F) // Y
    rows = part // CUTS
    count = F * pairs
    around = Y * per_dev
    frontal = frontal_tiles.reshape(per_dev, Y, part, width)
    n = CHUNKS

    def f32(*shape):
        return pltpu.VMEM(shape, jnp.float32)

    def i16(*shape):
        return pltpu.VMEM(shape, jnp.int16)

    dma = pltpu.SemaphoreType.DMA
    scratch = [
        pltpu.SMEM((pairs,), jnp.int32),
        pltpu.SMEM((pairs,), jnp.int32),
        pltpu.SMEM(reader_tile.shape, jnp.int32),
        pltpu.VMEM(left.shape, left.dtype),
        pltpu.VMEM(right.shape, right.dtype),
        f32(*frontal.shape),
        f32(*diag_inverse.shape),
        f32(2, pairs, depth * width, HALF),
        pltpu.VMEM((Y * F, 16, 128), jnp.int32),
        pltpu.VMEM((Y * 16, 128), jnp.int32),
        pltpu.SMEM((Y * 16, 128), jnp.int32),
        f32(Y, per_dev, part, width),
        f32(Y, per_dev, part, width),
        f32(Y, per_dev, part, width),
        f32(n, around * rows, HALF),
        i16(F * Y, n, pairs * rows, HALF),
        f32(F * Y, n, 1, HALF),
        i16(Y * F, n, pairs * rows, HALF),
        f32(Y * F, n, 1, HALF),
        f32(n, Z, around * rows, HALF),
        i16(Z, n, around * rows, HALF),
        f32(Z, n, 1, HALF),
        i16(Z - 1, n, around * rows, HALF),
        f32(Z - 1, n, 1, HALF),
        i16(Y - 1, n, listed * rows, HALF),
        f32(Y - 1, n, listed, 1, HALF),
        i16(Y, n, listed * rows, HALF),
        f32(Y, n, listed, 1, HALF),
        *[f32(count + 1, rows, HALF)] * Y,
        *[i16(Z, around * rows // 16, 16, HALF)] * n,
        *[f32(Z, 1, HALF)] * n,
        dma((2,)),
        dma((2, 2, n)),
        dma((2, 2, n)),
        dma((2, 2, n)),
        dma((2, 2, n)),
        dma((2,)),
        dma((2,)),
        dma((2, n)),
        dma,
        dma((7,)),
    ]
    hbm = pl.BlockSpec(memory_space=pltpu.HBM)
    vmem = pl.BlockSpec(memory_space=pltpu.VMEM)
    ancestor, picked = pl.pallas_call(
        kernel,
        out_shape=(
            pltpu.VMEM(frontal.shape, jnp.float32),
            pltpu.VMEM((listed,) + frontal.shape[1:], jnp.float32),
        ),
        in_specs=[hbm] * 7,
        out_specs=(vmem, vmem),
        scratch_shapes=scratch,
        compiler_params=pltpu.CompilerParams(
            collective_id=0, has_side_effects=True, vmem_limit_bytes=60 << 20
        ),
        cost_estimate=pl.CostEstimate(
            flops=2 * pairs * depth * width**3, bytes_accessed=4 << 20, transcendentals=0
        ),
        name="schur_update",
    )(dest_owner[0, :, 0], tile_slot[0], reader_tile, left, right, frontal, diag_inverse)
    return (
        ancestor.reshape(frontal_tiles.shape),
        picked.reshape((listed,) + frontal_tiles.shape[1:]),
    )


def solution(mesh):
    placed = (
        P("forest", "tile", None, None, None),
        P("forest", "tile", None, None, None),
        P("forest", "tile", None),
        P("forest", "tile"),
        P("tile", None, "forest", None),
        P(),
        P(),
    )
    return jax.shard_map(
        per_device,
        mesh=mesh,
        in_specs=placed,
        out_specs=(P("tile", None, "forest", None), P("tile", None, "forest", None)),
        check_vma=False,
    )
```

```python
import functools

import jax
import jax.numpy as jnp
from jax import lax
from jax.experimental import pallas as pl
from jax.experimental.pallas import tpu as pltpu
from jax.sharding import PartitionSpec as P

MESH = pl.DeviceIdType.MESH
Y = 4
Z = 8
F = 8
HALF = 128
CUTS = 1
CHUNKS = 2 * CUTS
TOP = 32767.0


def scale_of(v):
    v = jnp.abs(v)
    most = functools.reduce(jnp.maximum, [v[i:i + 8] for i in range(0, v.shape[0], 8)])
    most = jnp.maximum(jnp.max(most, axis=0, keepdims=True), 1e-30)
    return most * (1.0 / TOP), TOP / most


def encode(v):
    step, back = scale_of(v)
    return jnp.round(v * back).astype(jnp.int32).astype(jnp.int16), step


def decode(q, step):
    return q.astype(jnp.int32).astype(jnp.float32) * step


def kernel(
    owner_at, slot_at, reads_at, left_at, right_at, frontal_at, inverse_at, ancestor, picked, *scratch
):
    (owner, slot, reads, left, right, frontal, inverse, product, ids, meta_v, meta,
     front, parts, parts_in, solid, x_out, xs_out, x_in, xs_in, mine, z_out, zs_out, z_in, zs_in,
     r_out, rs_out, r_in, rs_in, *rest) = scratch
    sums, rest = rest[:Y], rest[Y:]
    g_all, rest = rest[:CHUNKS], rest[CHUNKS:]
    gs_all, rest = rest[:CHUNKS], rest[CHUNKS:]
    id_sem, x_sem, z_sem, g_sem, r_sem, f_sem, a_sem, own_sem, meta_sem, in_sem = rest

    loads = [
        pltpu.make_async_copy(src, dst, in_sem.at[i])
        for i, (src, dst) in enumerate([
            (left_at, left), (right_at, right), (owner_at, owner), (slot_at, slot),
            (reads_at, reads), (frontal_at, frontal), (inverse_at, inverse),
        ])
    ]
    for copy in loads:
        copy.start()

    pairs, depth, width = left.shape[:3]
    per_dev = frontal.shape[0]
    listed = picked.shape[0]
    part = frontal.shape[2]
    rows = part // CUTS
    count = F * pairs
    around = Y * per_dev
    f = lax.axis_index("forest")
    t = lax.axis_index("tile")
    z, y = t // Y, t % Y

    x_peers = [
        ((f + i) % F, z * Y + (y + l) % Y) for l in range(Y) for i in range(F) if i or l
    ]
    y_peers = [(f, z * Y + (y + i) % Y) for i in range(1, Y)]
    z_peers = [(f, (z + i) % Z * Y + y) for i in range(1, Z)]
    barrier = pltpu.get_barrier_semaphore()
    for peer in x_peers + z_peers:
        pl.semaphore_signal(barrier, inc=1, device_id=peer, device_id_type=MESH)

    def send(src, dst, sems, at, peer):
        pltpu.make_async_remote_copy(
            src_ref=src, dst_ref=dst, send_sem=sems.at[(0,) + at], recv_sem=sems.at[(1,) + at],
            device_id=peer, device_id_type=MESH,
        ).start()

    def wait(way, like, sems, at):
        pltpu.make_async_copy(like, like, sems.at[(way,) + at]).wait()

    loads[2].wait()
    loads[3].wait()
    lane = lax.broadcasted_iota(jnp.int32, (1, 128), 1)
    along = jnp.zeros((1, 128), jnp.int32)
    for k in range(pairs):
        along = jnp.where(lane == f * pairs + k, owner[k] * per_dev + slot[k], along)
    ids[y * F + f] = along

    def block_of(ff, yy):
        return yy // 2 * (2 * F) + ff * 2 + yy % 2

    def multiply(col):
        def body(k, carry):
            b = right[k, 0, :, col * HALF:(col + 1) * HALF]
            for tile in range(depth):
                product[col, k, tile * width:(tile + 1) * width] = jnp.dot(
                    left[k, tile], b, preferred_element_type=jnp.float32
                )
            return carry

        lax.fori_loop(0, pairs, body, 0)

    last = F * Y - 1
    owns = {}

    def start_x(c):
        cut, col = c // 2, c % 2
        if cut == 0:
            multiply(col)

        def pack(b, carry):
            at = pl.multiple_of(b * part + cut * rows, 8)
            v = jnp.concatenate(
                [product[col, k, pl.ds(at, rows)] for k in range(pairs)], axis=0
            )
            x_out[b, c], xs_out[b, c] = encode(v)
            return carry

        lax.fori_loop(0, F * Y, pack, 0, unroll=4)
        if c == 0:
            pl.semaphore_wait(barrier, len(x_peers + z_peers))
        for peer in x_peers:
            b = block_of(peer[0], peer[1] % Y)
            send(x_out.at[b, c], x_in.at[y * F + f, c], x_sem, (0, c), peer)
            send(xs_out.at[b, c], xs_in.at[y * F + f, c], x_sem, (1, c), peer)
        b = block_of(f, y)
        owns[c] = [
            pltpu.make_async_copy(x_out.at[b, c], x_in.at[y * F + f, c], own_sem.at[0, c]),
            pltpu.make_async_copy(xs_out.at[b, c], xs_in.at[y * F + f, c], own_sem.at[1, c]),
        ]
        for copy in owns[c]:
            copy.start()

    loads[0].wait()
    loads[1].wait()
    start_x(0)
    for peer in x_peers:
        send(ids.at[y * F + f], ids.at[y * F + f], id_sem, (), peer)
    for copy in loads[4:]:
        copy.wait()
    for peer in y_peers:
        send(frontal.at[:, peer[1] % Y], front.at[y], f_sem, (), peer)
    front[y] = frontal[:, y]
    for c in range(1, CHUNKS):
        start_x(c)

    wait(1, ids.at[pl.ds(0, last)], id_sem, ())
    number = lax.broadcasted_iota(jnp.int32, (count, 128), 0)
    place = lax.broadcasted_iota(jnp.int32, (count, 128), 1)

    def latest(mask):
        at = jnp.max(jnp.where(mask, number, -1), axis=0, keepdims=True)
        return jnp.broadcast_to(jnp.where(at < 0, count, at), (8, 128))

    for yy in range(Y):
        line = sum(ids[yy * F + ff] for ff in range(F))
        line = jnp.broadcast_to(line, (count, 128))
        cols = jnp.sum(jnp.where(number == place, line, 0), axis=1, keepdims=True)
        cols = jnp.broadcast_to(cols, (count, 128))
        meta_v[yy * 16:yy * 16 + 8, :] = latest((cols == line) & (number < place))
        meta_v[yy * 16 + 8:yy * 16 + 16, :] = latest(cols == place)
        sums[yy][count] = jnp.zeros((rows, HALF), jnp.float32)
    copy = pltpu.make_async_copy(meta_v, meta, meta_sem)
    copy.start()
    copy.wait()

    def start_z(c):
        wait(1, x_in.at[pl.ds(0, last), c], x_sem, (0, c))
        wait(1, xs_in.at[pl.ds(0, last), c], x_sem, (1, c))
        for copy in owns[c]:
            copy.wait()

        def chain(ff, carry):
            values = [decode(x_in[yy * F + ff, c], xs_in[yy * F + ff, c]) for yy in range(Y)]
            for k in range(pairs):
                j = ff * pairs + k
                for yy in range(Y):
                    earlier = sums[yy][meta[yy * 16, j]]
                    sums[yy][j] = values[yy][k * rows:(k + 1) * rows] + earlier
            return carry

        lax.fori_loop(0, F, chain, 0, unroll=2)

        def pack(zz, carry):
            values = []
            for m in range(around):
                g = zz * around + m
                values.append(sum(sums[yy][meta[yy * 16 + 8, g]] for yy in range(Y)))
            v = jnp.concatenate(values, axis=0)
            mine[c, zz] = v
            z_out[zz, c], zs_out[zz, c] = encode(v)
            return carry

        lax.fori_loop(0, Z, pack, 0, unroll=2)
        for i, peer in enumerate(z_peers):
            to = (z + i + 1) % Z
            send(z_out.at[to, c], z_in.at[i, c], z_sem, (0, c), peer)
            send(zs_out.at[to, c], zs_in.at[i, c], z_sem, (1, c), peer)

    def dot(a, b):
        return jnp.dot(
            a, b, precision=lax.Precision.HIGHEST, preferred_element_type=jnp.float32
        )

    def start_g(c):
        cut, col = c // 2, c % 2
        at = slice(cut * rows, (cut + 1) * rows)
        cols = slice(col * HALF, (col + 1) * HALF)
        if c == 0:
            wait(1, front.at[pl.ds(0, Y - 1)], f_sem, ())
        wait(1, z_in.at[:, c], z_sem, (0, c))
        wait(1, zs_in.at[:, c], z_sem, (1, c))
        v = mine[c, z]
        for i in range(Z - 1):
            v = v + decode(z_in[i, c], zs_in[i, c])
        before = [front[m // per_dev, m % per_dev, at, cols] for m in range(around)]
        v = jnp.concatenate(before, axis=0) - v * (1.0 / depth)
        solid[c] = v
        for m in range(around):
            parts[m // per_dev, m % per_dev, at, cols] = v[m * rows:(m + 1) * rows]
        solved = dot(v, inverse[cols, cols])
        if col:
            solved = solved + dot(solid[c - 1], inverse[0:HALF, cols])
        q, step = encode(solved)
        for m in range(around * rows // 16):
            g_all[c][z, m] = q[m * 16:(m + 1) * 16]
        gs_all[c][z] = step
        for peer in z_peers:
            send(g_all[c].at[z], g_all[c].at[z], g_sem, (0, c), peer)
            send(gs_all[c].at[z], gs_all[c].at[z], g_sem, (1, c), peer)
        if c == CHUNKS - 1:
            for peer in y_peers:
                send(parts.at[peer[1] % Y], parts_in.at[y], a_sem, (), peer)
            parts_in[y] = parts[y]

    def start_r(c):
        wait(1, g_all[c].at[pl.ds(0, Z - 1)], g_sem, (0, c))
        wait(1, gs_all[c].at[pl.ds(0, Z - 1)], g_sem, (1, c))
        for i in range(Y):
            to = (y + i) % Y
            values = []
            for r in range(listed):
                g = reads[(z * Y + to) * listed + r]
                at = g % around
                if rows == 16:
                    q = g_all[c][g // around, at].astype(jnp.int32)
                else:
                    q = g_all[c][g // around, at // 2].astype(jnp.int32)
                    q = jnp.where(at % 2 == 1, q[8:16], q[0:8])
                values.append(q)
            q = jnp.concatenate(values, axis=0).astype(jnp.int16)
            for r in range(listed):
                g = reads[(z * Y + to) * listed + r]
                step = gs_all[c][g // around]
                if i == 0:
                    rs_in[y, c, r] = step
                else:
                    rs_out[i - 1, c, r] = step
            if i == 0:
                r_in[y, c] = q
                continue
            r_out[i - 1, c] = q
            peer = y_peers[i - 1]
            send(r_out.at[i - 1, c], r_in.at[y, c], r_sem, (0, c), peer)
            send(rs_out.at[i - 1, c], rs_in.at[y, c], r_sem, (1, c), peer)

    def finish(c):
        cut, col = c // 2, c % 2
        wait(1, r_in.at[pl.ds(0, Y - 1), c], r_sem, (0, c))
        wait(1, rs_in.at[pl.ds(0, Y - 1), c], r_sem, (1, c))
        for yy in range(Y):
            q = r_in[yy, c].astype(jnp.int32).astype(jnp.float32)
            for r in range(listed):
                picked[r, yy, cut * rows:(cut + 1) * rows, col * HALF:(col + 1) * HALF] = (
                    q[r * rows:(r + 1) * rows] * rs_in[yy, c, r]
                )

    stages = (start_z, start_g, start_r, finish)
    for wave in range(CHUNKS + len(stages) - 1):
        for number_of, stage in reversed(list(enumerate(stages))):
            if 0 <= wave - number_of < CHUNKS:
                stage(wave - number_of)

    wait(1, parts_in.at[pl.ds(0, Y - 1)], a_sem, ())
    for yy in range(Y):
        for s in range(per_dev):
            ancestor[s, yy] = parts_in[yy, s]
    wait(0, ids.at[pl.ds(0, last)], id_sem, ())
    wait(0, front.at[pl.ds(0, Y - 1)], f_sem, ())
    wait(0, parts.at[pl.ds(0, Y - 1)], a_sem, ())
    for c in range(CHUNKS):
        wait(0, x_out.at[pl.ds(0, last), c], x_sem, (0, c))
        wait(0, xs_out.at[pl.ds(0, last), c], x_sem, (1, c))
        wait(0, z_out.at[pl.ds(0, Z - 1), c], z_sem, (0, c))
        wait(0, zs_out.at[pl.ds(0, Z - 1), c], z_sem, (1, c))
        wait(0, g_all[c].at[pl.ds(0, Z - 1)], g_sem, (0, c))
        wait(0, gs_all[c].at[pl.ds(0, Z - 1)], g_sem, (1, c))
        wait(0, r_out.at[:, c], r_sem, (0, c))
        wait(0, rs_out.at[:, c], r_sem, (1, c))


def per_device(
    left_panels, right_panels, dest_owner, tile_slot, frontal_tiles, diag_inverse, reader_tile
):
    left = left_panels[0]
    right = right_panels[0]
    pairs, depth, width = left.shape[:3]
    per_dev = frontal_tiles.shape[0]
    listed = reader_tile.shape[0] // lax.axis_size("tile")
    part = depth * (width // F) // Y
    rows = part // CUTS
    count = F * pairs
    around = Y * per_dev
    frontal = frontal_tiles.reshape(per_dev, Y, part, width)
    n = CHUNKS

    def f32(*shape):
        return pltpu.VMEM(shape, jnp.float32)

    def i16(*shape):
        return pltpu.VMEM(shape, jnp.int16)

    dma = pltpu.SemaphoreType.DMA
    scratch = [
        pltpu.SMEM((pairs,), jnp.int32),
        pltpu.SMEM((pairs,), jnp.int32),
        pltpu.SMEM(reader_tile.shape, jnp.int32),
        pltpu.VMEM(left.shape, left.dtype),
        pltpu.VMEM(right.shape, right.dtype),
        f32(*frontal.shape),
        f32(*diag_inverse.shape),
        f32(2, pairs, depth * width, HALF),
        pltpu.VMEM((Y * F, 1, 128), jnp.int32),
        pltpu.VMEM((Y * 16, 128), jnp.int32),
        pltpu.SMEM((Y * 16, 128), jnp.int32),
        f32(Y, per_dev, part, width),
        f32(Y, per_dev, part, width),
        f32(Y, per_dev, part, width),
        f32(n, around * rows, HALF),
        i16(F * Y, n, pairs * rows, HALF),
        f32(F * Y, n, 1, HALF),
        i16(Y * F, n, pairs * rows, HALF),
        f32(Y * F, n, 1, HALF),
        f32(n, Z, around * rows, HALF),
        i16(Z, n, around * rows, HALF),
        f32(Z, n, 1, HALF),
        i16(Z - 1, n, around * rows, HALF),
        f32(Z - 1, n, 1, HALF),
        i16(Y - 1, n, listed * rows, HALF),
        f32(Y - 1, n, listed, 1, HALF),
        i16(Y, n, listed * rows, HALF),
        f32(Y, n, listed, 1, HALF),
        *[f32(count + 1, rows, HALF)] * Y,
        *[i16(Z, around * rows // 16, 16, HALF)] * n,
        *[f32(Z, 1, HALF)] * n,
        dma((2,)),
        dma((2, 2, n)),
        dma((2, 2, n)),
        dma((2, 2, n)),
        dma((2, 2, n)),
        dma((2,)),
        dma((2,)),
        dma((2, n)),
        dma,
        dma((7,)),
    ]
    hbm = pl.BlockSpec(memory_space=pltpu.HBM)
    vmem = pl.BlockSpec(memory_space=pltpu.VMEM)
    ancestor, picked = pl.pallas_call(
        kernel,
        out_shape=(
            pltpu.VMEM(frontal.shape, jnp.float32),
            pltpu.VMEM((listed,) + frontal.shape[1:], jnp.float32),
        ),
        in_specs=[hbm] * 7,
        out_specs=(vmem, vmem),
        scratch_shapes=scratch,
        compiler_params=pltpu.CompilerParams(
            collective_id=0, has_side_effects=True, vmem_limit_bytes=60 << 20
        ),
        cost_estimate=pl.CostEstimate(
            flops=2 * pairs * depth * width**3, bytes_accessed=4 << 20, transcendentals=0
        ),
        name="schur_update",
    )(dest_owner[0, :, 0], tile_slot[0], reader_tile, left, right, frontal, diag_inverse)
    return (
        ancestor.reshape(frontal_tiles.shape),
        picked.reshape((listed,) + frontal_tiles.shape[1:]),
    )


def solution(mesh):
    placed = (
        P("forest", "tile", None, None, None),
        P("forest", "tile", None, None, None),
        P("forest", "tile", None),
        P("forest", "tile"),
        P("tile", None, "forest", None),
        P(),
        P(),
    )
    return jax.shard_map(
        per_device,
        mesh=mesh,
        in_specs=placed,
        out_specs=(P("tile", None, "forest", None), P("tile", None, "forest", None)),
        check_vma=False,
    )
```
